256 devices in a mesh: seq: 32 (over z, y_lo, core), tensor: 4 (over x), dp: 2 (over y_hi).
Axes of the slice: x: 4, y: 4 (y_hi: 2, y_lo: 2; y = y_hi * 2 + y_lo), z: 8, core: 2. Of those that a mesh axis runs over, the one named last changes fastest.
Arguments:
- queries: bfloat16 [2, 4096, 4096], P('dp', 'seq', 'tensor'), may hold values from -8 to 8
- neighbour_kv: bfloat16 [2, 16384, 2, 4096], P('dp', 'seq', None, 'tensor'), may hold values from -8 to 8
- block_target: int32 [2, 1024], P('dp', 'seq'), may hold values from 0 to 1023, as said below
- neighbour_count: int32 [2, 64], P('dp'), may hold values from 1 to 2
- out_weight: bfloat16 [32, 128, 4096], P('tensor', None, 'dp'), may hold values from -0.09375 to 0.09375
- grad_mixed: bfloat16 [2, 4096, 4096], P('dp', 'seq', 'tensor'), may hold values from -6 to 6
Outputs:
- layer_out: bfloat16 [2, 4096, 4096], P('dp', 'seq', 'tensor')
- grad_queries: bfloat16 [2, 4096, 4096], P('dp', 'seq', 'tensor')
- grad_kv: bfloat16 [2, 16384, 2, 4096], P('dp', 'seq', None, 'tensor')
- grad_out_weight: float32 [32, 128, 4096], P('tensor', 'seq', 'dp')
The draws below stay inside these ranges and needn't reach their ends.
Inputs may be any that keep to these rules, and one draw needn't show every extreme that they name: `block_target`: for each replica the entries are a permutation; the 32 blocks of one device's rows name exactly one of the blocks (b * 32 to b * 32 + 31) of each seq index b.
All inputs are finite; a program needn't handle non-finite values.
Results may differ from the reference program's by a relative error of at most 0.035.
Values may be sent and summed in bfloat16 or wider, within the bound.
No kernel may reach another device: no remote copies, remote signals or barrier semaphores. Data moves between devices by JAX's collectives and lax.ppermute only.
A program may use at most 128 MiB of HBM per device.

```python
import jax
import jax.numpy as jnp
from jax import lax

D = 4096
HEADS = 32
HD = 128
CLEN = 64
NLEN = 128
NEIGH = 2
INNER = 4096
SHARDS = 32
REPLICAS = 2
TOKENS = 4096
SPANS = 64
BLK = 16
BLOCKS = 1024
NB_TOTAL = 16384


def draw_queries(key, part):
    key = jax.random.fold_in(key, 11)
    values = jax.random.normal(key, (REPLICAS, TOKENS, INNER), jnp.float32)
    return jnp.clip(values, -8.0, 8.0).astype(jnp.bfloat16)


def draw_neighbour_kv(key, part):
    key = jax.random.fold_in(key, 13)
    values = jax.random.normal(key, (REPLICAS, NB_TOTAL, 2, INNER), jnp.float32)
    return jnp.clip(values, -8.0, 8.0).astype(jnp.bfloat16)


def draw_block_target(key, part):
    key = jax.random.fold_in(key, 23)

    def one_table(replica_key):
        owner_keys = jax.random.split(jax.random.fold_in(replica_key, 1), SHARDS)
        slot_keys = jax.random.split(jax.random.fold_in(replica_key, 2), SHARDS)
        owner_slot = jax.vmap(lambda single: jax.random.permutation(single, SHARDS))(owner_keys)
        dest_slot = jax.vmap(lambda single: jax.random.permutation(single, SHARDS))(slot_keys)
        entries = (jnp.arange(SHARDS)[None, :] * SHARDS + dest_slot.T).astype(jnp.int32)
        owners = jnp.broadcast_to(jnp.arange(SHARDS)[:, None], (SHARDS, SHARDS))
        table = jnp.zeros((SHARDS, SHARDS), jnp.int32).at[owners, owner_slot].set(entries)
        return table.reshape(BLOCKS)
    return jax.vmap(one_table)(jax.random.split(key, REPLICAS))


def place_ends(result, own_key, low, largest):
    longest = result.shape.index(max(result.shape))
    spots = []
    for shift in (0, 1):
        where = [jax.random.randint(jax.random.fold_in(own_key, axis), (), 0, length) for axis, length in enumerate(result.shape)]
        where[longest] = (where[longest] + shift) % result.shape[longest]
        spots.append(tuple(where))
    return result.at[spots[0]].set(low).at[spots[1]].set(largest)


def level_of(own_key, extent, cuts, least, largest):
    def one(axis_at, shards_of):
        heights = jax.random.uniform(jax.random.fold_in(jax.random.fold_in(own_key, 6), axis_at), (shards_of,), jnp.float32, least / len(cuts), largest / len(cuts))
        return jnp.repeat(jnp.exp(heights), extent[axis_at] // shards_of).reshape((-1,) + (1,) * (len(extent) - axis_at - 1))

    level = one(*cuts[0])
    for cut in cuts[1:]:
        level = level * one(*cut)
    return level


def scatter_about(stream_key, dims, spread, bound, shards=(), held_as=jnp.bfloat16):
    result = spread * jax.random.normal(stream_key, dims, jnp.float32)
    if shards:
        result = result * level_of(stream_key, dims, shards, -0.22, 0.18)
    return jnp.clip(result, -bound, bound).astype(held_as)


def setup_inputs(seed: int = 0) -> dict:
    seeds = jax.random.split(jax.random.key(seed), 7)
    return {
        "queries": draw_queries(jax.random.fold_in(seeds[6], 71), 0),
        "neighbour_kv": draw_neighbour_kv(jax.random.fold_in(seeds[6], 71), 0),
        "block_target": draw_block_target(jax.random.fold_in(seeds[6], 71), 0),
        "neighbour_count": place_ends(jax.random.randint(seeds[3], (REPLICAS, SPANS), 1, 3), jax.random.fold_in(seeds[3], 1), 1, 2).astype(jnp.int32),
        "out_weight": scatter_about(seeds[4], (HEADS, HD, D), INNER ** -0.5, 0.09375, ((0, 4), (2, 2))),
        "grad_mixed": scatter_about(seeds[5], (REPLICAS, TOKENS, D), 1.0, 6.0, ((0, 2), (1, 32), (2, 4))),
    }


NEG_FILL = -1e30


def attend_window(query_win, kv_win, key_live):
    score_scale = HD ** -0.5
    query_heads = query_win.astype(jnp.float32).reshape(CLEN, HEADS, HD)
    key_heads = kv_win[:, 0].astype(jnp.float32).reshape(NEIGH * NLEN, HEADS, HD)
    value_heads = kv_win[:, 1].astype(jnp.float32).reshape(NEIGH * NLEN, HEADS, HD)
    scores = jnp.einsum("qhd,khd->hqk", query_heads, key_heads) * score_scale
    scores = jnp.where(key_live[None, None, :], scores, NEG_FILL)
    row_top = jnp.max(scores, axis=-1, keepdims=True)
    raw_weights = jnp.exp(scores - row_top)
    soft_weights = raw_weights / jnp.sum(raw_weights, axis=-1, keepdims=True)
    low_weights = lax.optimization_barrier(soft_weights.astype(jnp.bfloat16)).astype(jnp.float32)
    context = jnp.einsum("hqk,khd->qhd", low_weights, value_heads).reshape(CLEN, INNER).astype(jnp.bfloat16)
    return context, soft_weights, low_weights, query_heads, key_heads, value_heads


def window_forward(window_items):
    return attend_window(window_items[0], window_items[1], window_items[2])[0]


def window_backward(window_items):
    query_win, kv_win, key_live, grad_win = window_items
    score_scale = HD ** -0.5
    context, soft_weights, low_weights, query_heads, key_heads, value_heads = attend_window(query_win, kv_win, key_live)
    grad_heads = grad_win.astype(jnp.float32).reshape(CLEN, HEADS, HD)
    grad_value = jnp.einsum("hqk,qhd->khd", low_weights, grad_heads)
    grad_weights = jnp.einsum("qhd,khd->hqk", grad_heads, value_heads)
    row_delta = jnp.einsum("qhd,qhd->hq", grad_heads, context.astype(jnp.float32).reshape(CLEN, HEADS, HD))[..., None]
    grad_scores = soft_weights * (grad_weights - row_delta)
    grad_query = jnp.einsum("hqk,khd->qhd", grad_scores, key_heads) * score_scale
    grad_key = jnp.einsum("hqk,qhd->khd", grad_scores, query_heads) * score_scale
    stacked = jnp.stack([grad_key, grad_value], axis=1).reshape(NEIGH * NLEN, 2, INNER)
    return grad_query.reshape(CLEN, INNER), stacked


def one_replica(query_rows, kv_rows, table, counts, weight_mat, grad_out):
    table = table.astype(jnp.int32)
    blocks = kv_rows.reshape(BLOCKS, BLK, 2, INNER)
    arranged = blocks[jnp.argsort(table).astype(jnp.int32)].reshape(SPANS, NEIGH * NLEN, 2, INNER)
    key_live = jnp.arange(NEIGH * NLEN)[None, :] < (counts * NLEN)[:, None]
    query_ext = jnp.concatenate([query_rows, jnp.zeros((CLEN, INNER), jnp.bfloat16)], axis=0)
    windows = query_ext[CLEN - 1:CLEN - 1 + TOKENS].reshape(SPANS, CLEN, INNER)
    ctx_windows = lax.map(window_forward, (windows, arranged, key_live))
    context = jnp.concatenate([jnp.zeros((CLEN - 1, INNER), jnp.bfloat16),
                               ctx_windows.reshape(TOKENS, INNER)[:TOKENS - CLEN + 1]], axis=0)
    layer_out = jnp.dot(context, weight_mat, preferred_element_type=jnp.float32).astype(jnp.bfloat16)
    grad_context = jnp.dot(grad_out, weight_mat.T, preferred_element_type=jnp.float32).astype(jnp.bfloat16)
    weight_grad = jnp.dot(context.T, grad_out, preferred_element_type=jnp.float32)
    grad_ext = jnp.concatenate([grad_context, jnp.zeros((CLEN, INNER), jnp.bfloat16)], axis=0)
    grad_windows = grad_ext[CLEN - 1:CLEN - 1 + TOKENS].reshape(SPANS, CLEN, INNER)
    grad_query_win, grad_kv_win = lax.map(window_backward, (windows, arranged, key_live, grad_windows))
    grad_queries = jnp.concatenate([jnp.zeros((CLEN - 1, INNER), jnp.float32),
                                    grad_query_win.reshape(TOKENS, INNER)[:TOKENS - CLEN + 1]], axis=0).astype(jnp.bfloat16)
    grad_blocks = grad_kv_win.astype(jnp.bfloat16).reshape(BLOCKS, BLK, 2, INNER)[table]
    return layer_out, grad_queries, grad_blocks.reshape(NB_TOTAL, 2, INNER), weight_grad


def reference(queries, neighbour_kv, block_target, neighbour_count, out_weight, grad_mixed):
    weight_mat = out_weight.reshape(INNER, D)
    results = []
    for replica in range(REPLICAS):
        results.append(one_replica(queries[replica], neighbour_kv[replica], block_target[replica],
                                   neighbour_count[replica], weight_mat, grad_mixed[replica]))
    weight_total = results[0][3]
    for replica in range(1, REPLICAS):
        weight_total = weight_total + results[replica][3]
    return (jnp.stack([entry[0] for entry in results]), jnp.stack([entry[1] for entry in results]),
            jnp.stack([entry[2] for entry in results]), weight_total.reshape(HEADS, HD, D))
```

```python
import functools

import jax
import jax.numpy as jnp
from jax import lax
from jax.experimental import pallas as pl
from jax.experimental.pallas import tpu as pltpu
from jax.sharding import PartitionSpec as P

CLEN = 64
NLEN = 128
HD = 128
BLK = 16
SHARDS = 32
TENSOR = 4
REPLICAS = 2
NEG_FILL = -1e30
CHUNKS = 2
AXES = ("seq", "tensor", "dp")


def moved(value, where):
    pairs = []
    for s in range(SHARDS):
        for t in range(TENSOR):
            for d in range(REPLICAS):
                to = where(s, t, d)
                if to is not None:
                    pairs.append(((s * TENSOR + t) * REPLICAS + d, (to[0] * TENSOR + to[1]) * REPLICAS + to[2]))
    return lax.ppermute(value, AXES, pairs)


def to_previous(value):
    return moved(value, lambda s, t, d: (s - 1, t, d) if s > 0 else None)


def to_next(value):
    return moved(value, lambda s, t, d: (s + 1, t, d) if s + 1 < SHARDS else None)


def flip_seq(value, bits):
    return moved(value, lambda s, t, d: (s ^ bits, t, d))


def flip_dp(value):
    return moved(value, lambda s, t, d: (s, t, 1 - d))


def pick(index, options):
    chosen = options[-1]
    for at in range(len(options) - 2, -1, -1):
        chosen = jnp.where(index == at, options[at], chosen)
    return chosen


def to_windows(rows):
    half = rows.shape[0] // 2
    after = to_previous(rows[:half])
    own = lax.broadcasted_iota(jnp.int32, (half, 1), 0) == half - 1
    return jnp.concatenate([rows[half:], jnp.where(own, rows[:half], after)], axis=0)


def from_windows(rows):
    half = rows.shape[0] // 2
    before = to_next(rows[half:])
    own = lax.broadcasted_iota(jnp.int32, (half, 1), 0) == half - 1
    return jnp.concatenate([jnp.where(own, rows[half:], before), rows[:half]], axis=0)


def attend_kernel(bias_ref, query_ref, grad_ref, kv_ref, grad_kv_ref, context_ref, grad_query_ref):
    rows, size = query_ref.shape
    blocks = kv_ref.shape[0]
    keys = blocks * BLK
    scale = size ** (-0.5)
    query = query_ref[...]
    grad = grad_ref[...]
    key = kv_ref[:, :BLK, :].reshape(keys, size)
    value = kv_ref[:, BLK:, :].reshape(keys, size)
    row = lax.broadcasted_iota(jnp.int32, (rows, 1), 0)
    second = (row >= CLEN - 1) & (row < rows - 1)
    bias = jnp.where(second, bias_ref[1:2, :], bias_ref[0:1, :])
    nt = (((1,), (1,)), ((), ()))
    tn = (((0,), (0,)), ((), ()))
    scores = lax.dot_general(query, key, nt, preferred_element_type=jnp.float32) * scale + bias
    raw = jnp.exp(scores - jnp.max(scores, axis=-1, keepdims=True))
    soft = raw * (1.0 / jnp.sum(raw, axis=-1, keepdims=True))
    low = soft.astype(jnp.bfloat16)
    context = jnp.dot(low, value, preferred_element_type=jnp.float32).astype(jnp.bfloat16)
    context_ref[...] = context
    grad_weights = lax.dot_general(grad, value, nt, preferred_element_type=jnp.float32)
    delta = jnp.sum(grad.astype(jnp.float32) * context.astype(jnp.float32), axis=-1, keepdims=True)
    grad_scores = (soft * (grad_weights - delta) * scale).astype(jnp.bfloat16)
    grad_query_ref[...] = jnp.dot(grad_scores, key, preferred_element_type=jnp.float32).astype(jnp.bfloat16)
    grad_key = lax.dot_general(grad_scores, query, tn, preferred_element_type=jnp.float32)
    grad_value = lax.dot_general(low, grad, tn, preferred_element_type=jnp.float32)
    grad_kv_ref[:, :BLK, :] = grad_key.astype(jnp.bfloat16).reshape(blocks, BLK, size)
    grad_kv_ref[:, BLK:, :] = grad_value.astype(jnp.bfloat16).reshape(blocks, BLK, size)


def attend(bias, query, grad, kv, first_head):
    rows = query.shape[0]
    blocks, block_rows, width = kv.shape
    heads = width // HD
    per_head = pl.BlockSpec((rows, HD), lambda h: (0, h))
    shifted = pl.BlockSpec((rows, HD), lambda h: (0, h + first_head))
    block_spec = pl.BlockSpec((blocks, block_rows, HD), lambda h: (0, 0, h))
    keys = blocks * BLK
    return pl.pallas_call(
        attend_kernel,
        grid=(heads,),
        in_specs=[pl.BlockSpec((2, keys), lambda h: (0, 0)), shifted, shifted, block_spec],
        out_specs=[block_spec, per_head, per_head],
        out_shape=[
            jax.ShapeDtypeStruct(kv.shape, jnp.bfloat16),
            jax.ShapeDtypeStruct((rows, width), jnp.bfloat16),
            jax.ShapeDtypeStruct((rows, width), jnp.bfloat16),
        ],
        compiler_params=pltpu.CompilerParams(vmem_limit_bytes=32 * 1024 * 1024),
        cost_estimate=pl.CostEstimate(
            flops=heads * 12 * rows * keys * HD,
            bytes_accessed=4 * kv.size + 8 * rows * width,
            transcendentals=heads * rows * keys,
        ),
    )(bias, query, grad, kv)


def summed_over_z(parts, seq_place):
    z = seq_place // 4
    kept = parts
    for bit in range(3):
        mine = (z >> bit) & 1
        pairs = kept.reshape((kept.shape[0] // 2, 2) + kept.shape[1:])
        keep = jnp.where(mine == 0, pairs[:, 0], pairs[:, 1])
        send = jnp.where(mine == 0, pairs[:, 1], pairs[:, 0]).astype(jnp.bfloat16)
        kept = keep + flip_seq(send, 4 << bit).astype(jnp.float32)
    return kept[0]


def local(queries, neighbour_kv, block_target, neighbour_count, out_weight, grad_mixed):
    seq_place = lax.axis_index("seq")
    tensor_place = lax.axis_index("tensor")
    dp_place = lax.axis_index("dp")
    core = seq_place % 2
    pair = (seq_place // 2) % 2
    rows, inner_dev = queries.shape[1:]
    heads_dev = inner_dev // HD
    chunk_width = inner_dev // CHUNKS

    target = block_target[0]
    destination = target // SHARDS
    matches = destination[None, :] == jnp.arange(SHARDS)[:, None]
    send_order = jnp.sum(jnp.where(matches, jnp.arange(SHARDS)[None, :], 0), axis=1)
    blocks = neighbour_kv[0].reshape(SHARDS, BLK, 2, inner_dev).transpose(0, 2, 1, 3)
    outgoing = blocks.reshape(SHARDS, 2 * BLK, inner_dev)[send_order]
    incoming = [
        lax.all_to_all(
            outgoing[:, :, at * chunk_width : (at + 1) * chunk_width], "seq", split_axis=0, concat_axis=0, tiled=True
        )
        for at in range(CHUNKS)
    ]
    targets_all = lax.all_gather(target, "seq", axis=0, tiled=False)
    mine = targets_all // SHARDS == seq_place
    slot = jnp.sum(jnp.where(mine, targets_all % SHARDS, 0), axis=1)
    counts = lax.dynamic_slice(neighbour_count[0], (2 * seq_place,), (2,))
    live = (slot[None, :] // 16 == jnp.arange(2)[:, None]) & (slot[None, :] % 16 // 8 < counts[:, None])
    bias = jnp.where(jnp.repeat(live, BLK, axis=1), 0.0, NEG_FILL).astype(jnp.float32)

    query_rows = to_windows(queries[0])
    grad_rows = to_windows(grad_mixed[0])
    rounds = [
        moved(grad_rows, lambda s, t, d, j=j: (s, (2 * d + t % 2) ^ j, t // 2)) for j in range(4)
    ]
    quarter = [pick(tensor_place ^ at, rounds) for at in range(4)]
    weight = out_weight.reshape(inner_dev, -1)
    grad_half = jnp.concatenate(
        [jnp.concatenate(quarter[:2], axis=1), jnp.concatenate(quarter[2:], axis=1)], axis=0
    )
    partial_grad = lax.dot_general(
        grad_half, weight, (((1,), (1,)), ((), ())), preferred_element_type=jnp.float32
    ).reshape(2, rows, inner_dev)
    grad_own = jnp.where(dp_place == 0, partial_grad[0], partial_grad[1])
    grad_other = jnp.where(dp_place == 0, partial_grad[1], partial_grad[0]).astype(jnp.bfloat16)
    grad_context = (grad_own + flip_dp(grad_other).astype(jnp.float32)).astype(jnp.bfloat16)

    columns = [grad_half[:, : grad_half.shape[1] // 2], grad_half[:, grad_half.shape[1] // 2 :]]
    columns_own = jnp.where(core == 0, columns[0], columns[1])
    columns_other = jnp.where(core == 0, columns[1], columns[0])
    grad_group = jnp.concatenate(
        [columns_own, flip_seq(columns_other, 1), flip_seq(columns_own, 2), flip_seq(columns_other, 3)], axis=0
    )

    grad_blocks, contexts, grad_query_parts, weight_parts = [], [], [], []
    for at in range(CHUNKS):
        sent_back, context, grad_query = attend(bias, query_rows, grad_context, incoming[at], at * heads_dev // CHUNKS)
        grad_blocks.append(lax.all_to_all(sent_back, "seq", split_axis=0, concat_axis=0, tiled=True))
        grad_query_parts.append(grad_query)
        context_other = flip_dp(context)
        both = jnp.concatenate(
            [jnp.where(dp_place == 0, context, context_other), jnp.where(dp_place == 0, context_other, context)], axis=0
        )
        contexts.append(both)
        half = chunk_width // 2
        half_own = jnp.where(pair == 0, both[:, :half], both[:, half:])
        half_other = jnp.where(pair == 0, both[:, half:], both[:, :half])
        context_group = jnp.concatenate(
            [half_own, flip_seq(half_own, 1), flip_seq(half_other, 2), flip_seq(half_other, 3)], axis=0
        )
        terms = lax.dot_general(
            context_group, grad_group, (((0,), (0,)), ((), ())), preferred_element_type=jnp.float32
        )
        terms = terms.reshape(half // HD, 8, HD // 8, -1).transpose(1, 0, 2, 3)
        weight_parts.append(summed_over_z(terms, seq_place))

    weight_sum = jnp.stack(weight_parts, axis=0)
    weight_sum = weight_sum.reshape(weight_sum.shape[:2] + (4, 4, weight_sum.shape[-1]))
    place = 2 * pair + core
    received = [
        pick(place, [weight_sum[:, :, at] for at in range(4)])
    ] + [
        flip_seq(pick(place ^ bits, [weight_sum[:, :, at] for at in range(4)]), bits) for bits in (1, 2, 3)
    ]
    by_pair = []
    for p in range(2):
        by_core = [pick((2 * p + c) ^ place, received) for c in range(2)]
        by_pair.append(jnp.concatenate(by_core, axis=-1))
    weight_grad = jnp.stack(by_pair, axis=1).reshape(heads_dev, 4, -1)

    context_both = jnp.concatenate(contexts, axis=1)
    partial_out = jnp.dot(context_both, weight, preferred_element_type=jnp.float32).astype(jnp.bfloat16)
    width = partial_out.shape[1] // 2
    total = None
    for j in range(4):
        piece = tensor_place ^ j
        sent = lax.dynamic_slice(partial_out, (piece // 2 * rows, piece % 2 * width), (rows, width))
        came = moved(sent, lambda s, t, d, j=j: (s, 2 * d + (t ^ j) % 2, (t ^ j) // 2)).astype(jnp.float32)
        total = came if total is None else total + came
    layer_out = from_windows(total.astype(jnp.bfloat16))
    grad_queries = from_windows(jnp.concatenate(grad_query_parts, axis=1))

    returned = jnp.concatenate(grad_blocks, axis=2)[destination]
    grad_kv = returned.reshape(SHARDS, 2, BLK, inner_dev).transpose(0, 2, 1, 3)
    return (
        layer_out[None],
        grad_queries[None],
        grad_kv.reshape(1, SHARDS * BLK, 2, inner_dev),
        weight_grad,
    )


def solution(mesh):
    in_specs = (
        P("dp", "seq", "tensor"),
        P("dp", "seq", None, "tensor"),
        P("dp", "seq"),
        P("dp", None),
        P("tensor", None, "dp"),
        P("dp", "seq", "tensor"),
    )
    out_specs = (
        P("dp", "seq", "tensor"),
        P("dp", "seq", "tensor"),
        P("dp", "seq", None, "tensor"),
        P("tensor", "seq", "dp"),
    )
    return jax.shard_map(local, mesh=mesh, in_specs=in_specs, out_specs=out_specs, check_vma=False)
```

```python
import jax
import jax.numpy as jnp
from jax import lax
from jax.experimental import pallas as pl
from jax.experimental.pallas import tpu as pltpu
from jax.sharding import Mesh, PartitionSpec as P

CLEN = 64
NLEN = 128
HD = 128
BLK = 16
SHARDS = 32
TENSOR = 4
REPLICAS = 2
NEG_FILL = -1e30
STEPS = 4
GROUP = 2
SEQ = ("z", "y", "core")
AXES = SEQ + ("tensor", "dp")
TAIL = 8


def moved(value, where):
    pairs = []
    for s in range(SHARDS):
        for t in range(TENSOR):
            for d in range(REPLICAS):
                to = where(s, t, d)
                if to is not None:
                    pairs.append(((s * TENSOR + t) * REPLICAS + d, (to[0] * TENSOR + to[1]) * REPLICAS + to[2]))
    return lax.ppermute(value, AXES, pairs)


def to_previous(value):
    return moved(value, lambda s, t, d: (s - 1, t, d) if s > 0 else None)


def to_next(value):
    return moved(value, lambda s, t, d: (s + 1, t, d) if s + 1 < SHARDS else None)


def flip_seq(value, bits):
    return moved(value, lambda s, t, d: (s ^ bits, t, d))


def flip_tensor(value, bits):
    return moved(value, lambda s, t, d: (s, t ^ bits, d))


def flip_dp(value):
    return moved(value, lambda s, t, d: (s, t, 1 - d))


def pick(index, options):
    chosen = options[-1]
    for at in range(len(options) - 2, -1, -1):
        chosen = jnp.where(index == at, options[at], chosen)
    return chosen


def window_rows(own, after):
    half = after.shape[0]
    last = lax.broadcasted_iota(jnp.int32, (half, 1), 0) == half - 1
    return jnp.concatenate([own[-half:], jnp.where(last, own[-half - 1 : -half], after)], axis=0)


def token_rows(own, before):
    half = before.shape[0]
    last = lax.broadcasted_iota(jnp.int32, (half, 1), 0) == half - 1
    return jnp.concatenate([jnp.where(last, own[-1:], before), own[:half]], axis=0)


def split_kernel(query_ref, grad_ref, query_first_ref, grad_first_ref, grad_last_ref):
    half = query_first_ref.shape[0]
    query_first_ref[...] = query_ref[:half, :]
    grad_first_ref[...] = grad_ref[:half, :]
    grad_last_ref[...] = grad_ref[half - BLK :, :]


def split(query, grad):
    rows, width = query.shape
    vmem = pl.BlockSpec(memory_space=pltpu.VMEM)
    return pl.pallas_call(
        split_kernel,
        in_specs=[vmem] * 2,
        out_specs=[vmem] * 3,
        out_shape=[
            jax.ShapeDtypeStruct((size, width), jnp.bfloat16) for size in (rows // 2, rows // 2, rows // 2 + BLK)
        ],
        compiler_params=pltpu.CompilerParams(vmem_limit_bytes=56 * 1024 * 1024),
        cost_estimate=pl.CostEstimate(flops=0, bytes_accessed=16 * rows * width, transcendentals=0),
    )(query, grad)


def pack_kernel(target_ref, rows_ref, out_ref):
    step = pl.program_id(0)
    heads = rows_ref.shape[2] // HD
    blocks = rows_ref.shape[0] // BLK
    for at in range(blocks):
        target = target_ref[step * blocks + at]
        place = target // SHARDS
        for head in range(heads):
            pair = jnp.transpose(rows_ref[at * BLK : (at + 1) * BLK, :, head * HD : (head + 1) * HD], (1, 0, 2))
            row = 2 * BLK * head
            out_ref[place, row : row + BLK, :] = pair[0]
            out_ref[place, row + BLK : row + 2 * BLK, :] = pair[1]
        slot = jnp.full((TAIL, HD), target % SHARDS, jnp.int32)
        out_ref[place, 2 * BLK * heads :, :] = slot.astype(jnp.float32).astype(jnp.bfloat16)


def pack(target, rows):
    total, _, width = rows.shape
    out_rows = 2 * BLK * (width // HD) + TAIL
    return pl.pallas_call(
        pack_kernel,
        grid=(STEPS,),
        in_specs=[
            pl.BlockSpec(memory_space=pltpu.SMEM),
            pl.BlockSpec((total // STEPS, 2, width), lambda step: (step, 0, 0)),
        ],
        out_specs=pl.BlockSpec((SHARDS, out_rows, HD), lambda step: (0, 0, 0)),
        out_shape=jax.ShapeDtypeStruct((SHARDS, out_rows, HD), jnp.bfloat16),
        compiler_params=pltpu.CompilerParams(vmem_limit_bytes=56 * 1024 * 1024),
        cost_estimate=pl.CostEstimate(flops=0, bytes_accessed=16 * rows.size, transcendentals=0),
    )(target, rows)


def unpack_kernel(target_ref, part_ref, out_ref):
    step = pl.program_id(0)
    heads = out_ref.shape[2] // HD
    blocks = out_ref.shape[0] // BLK
    for at in range(blocks):
        source = target_ref[step * blocks + at] // SHARDS
        for head in range(heads):
            row = 2 * BLK * head
            both = part_ref[source, row : row + 2 * BLK, :].reshape(2, BLK, HD)
            out_ref[at * BLK : (at + 1) * BLK, :, head * HD : (head + 1) * HD] = jnp.transpose(both, (1, 0, 2))


def unpack(target, part):
    total, width = SHARDS * BLK, part.shape[1] // (2 * BLK) * HD
    return pl.pallas_call(
        unpack_kernel,
        grid=(STEPS,),
        in_specs=[
            pl.BlockSpec(memory_space=pltpu.SMEM),
            pl.BlockSpec(part.shape, lambda step: (0, 0, 0)),
        ],
        out_specs=pl.BlockSpec((total // STEPS, 2, width), lambda step: (step, 0, 0)),
        out_shape=jax.ShapeDtypeStruct((total, 2, width), jnp.bfloat16),
        compiler_params=pltpu.CompilerParams(vmem_limit_bytes=32 * 1024 * 1024),
        cost_estimate=pl.CostEstimate(flops=0, bytes_accessed=16 * total * width, transcendentals=0),
    )(target, part)


def attend_kernel(bias_ref, query_ref, grad_ref, kv_ref, grad_kv_ref, context_ref, grad_query_ref):
    rows = query_ref.shape[0]
    heads = query_ref.shape[1] // HD
    blocks = kv_ref.shape[0]
    keys = blocks * BLK
    scale = HD ** (-0.5)
    row = lax.broadcasted_iota(jnp.int32, (rows, 1), 0)
    second = (row >= CLEN - 1) & (row < rows - 1)
    bias = jnp.where(second, bias_ref[1:2, :], bias_ref[0:1, :])
    nt = (((1,), (1,)), ((), ()))
    tn = (((0,), (0,)), ((), ()))
    for head in range(heads):
        lanes = slice(head * HD, (head + 1) * HD)
        first, middle, last = 2 * BLK * head, 2 * BLK * head + BLK, 2 * BLK * (head + 1)
        query = query_ref[:, lanes]
        grad = grad_ref[:, lanes]
        key = kv_ref[:, first:middle, :].reshape(keys, HD)
        value = kv_ref[:, middle:last, :].reshape(keys, HD)
        scores = lax.dot_general(query, key, nt, preferred_element_type=jnp.float32) * scale + bias
        raw = jnp.exp(scores - jnp.max(scores, axis=-1, keepdims=True))
        soft = raw * (1.0 / jnp.sum(raw, axis=-1, keepdims=True))
        low = soft.astype(jnp.bfloat16)
        context = jnp.dot(low, value, preferred_element_type=jnp.float32).astype(jnp.bfloat16)
        context_ref[:, lanes] = context
        grad_weights = lax.dot_general(grad, value, nt, preferred_element_type=jnp.float32)
        delta = jnp.sum(grad.astype(jnp.float32) * context.astype(jnp.float32), axis=-1, keepdims=True)
        grad_scores = (soft * (grad_weights - delta) * scale).astype(jnp.bfloat16)
        grad_query = jnp.dot(grad_scores, key, preferred_element_type=jnp.float32)
        grad_query_ref[:, lanes] = grad_query.astype(jnp.bfloat16)
        grad_key = lax.dot_general(grad_scores, query, tn, preferred_element_type=jnp.float32)
        grad_value = lax.dot_general(low, grad, tn, preferred_element_type=jnp.float32)
        grad_kv_ref[:, first:middle, :] = grad_key.astype(jnp.bfloat16).reshape(blocks, BLK, HD)
        grad_kv_ref[:, middle:last, :] = grad_value.astype(jnp.bfloat16).reshape(blocks, BLK, HD)


def attend(bias, query, grad, kv):
    rows, width = query.shape
    blocks = kv.shape[0]
    keys = blocks * BLK
    heads = width // HD
    per_head = pl.BlockSpec((rows, GROUP * HD), lambda h: (0, h))
    block_spec = pl.BlockSpec((blocks, GROUP * 2 * BLK, HD), lambda h: (0, h, 0))
    return pl.pallas_call(
        attend_kernel,
        grid=(heads // GROUP,),
        in_specs=[pl.BlockSpec((2, keys), lambda h: (0, 0)), per_head, per_head, block_spec],
        out_specs=[block_spec, per_head, per_head],
        out_shape=[
            jax.ShapeDtypeStruct((blocks, 2 * BLK * heads, HD), jnp.bfloat16),
            jax.ShapeDtypeStruct((rows, width), jnp.bfloat16),
            jax.ShapeDtypeStruct((rows, width), jnp.bfloat16),
        ],
        compiler_params=pltpu.CompilerParams(vmem_limit_bytes=56 * 1024 * 1024),
        cost_estimate=pl.CostEstimate(
            flops=heads * 12 * rows * keys * HD,
            bytes_accessed=4 * kv.size + 8 * rows * width,
            transcendentals=heads * rows * keys,
        ),
    )(bias, query, grad, kv)


def local(queries, neighbour_kv, block_target, neighbour_count, out_weight, grad_mixed):
    seq_place = lax.axis_index(SEQ)
    tensor_place = lax.axis_index("tensor")
    dp_place = lax.axis_index("dp")
    core = seq_place % 2
    pair = (seq_place // 2) % 2
    rows, inner_dev = queries.shape[1:]
    heads_dev = inner_dev // HD

    half = rows // 2
    query_first, grad_first, grad_last = split(queries[0], grad_mixed[0])
    query_after = to_previous(query_first)
    grad_own = moved(grad_last, lambda s, t, d: (s, 2 * d + t % 2, t // 2))
    grad_after = moved(
        grad_first, lambda s, t, d: (s - 1, 2 * d + t % 2, t // 2) if s > 0 else None
    )
    packed = pack(block_target[0], neighbour_kv[0])
    packed, grad_own, grad_after, query_after = lax.optimization_barrier((packed, grad_own, grad_after, query_after))
    incoming = lax.all_to_all(packed, SEQ, split_axis=0, concat_axis=0, tiled=True)
    grad_rows = window_rows(grad_own, grad_after)
    rounds = [grad_rows] + [flip_tensor(grad_rows, bits) for bits in (1, 2, 3)]
    pair_rows = flip_seq(grad_rows, 2)
    pair_rows, rounds = lax.optimization_barrier((pair_rows, rounds))
    pair_rounds = [pair_rows] + [flip_tensor(pair_rows, bits) for bits in (1, 2, 3)]
    slot = incoming[:, -TAIL, 0].astype(jnp.int32)
    counts = lax.dynamic_slice(neighbour_count[0], (2 * seq_place,), (2,))
    live = (slot[None, :] // 16 == jnp.arange(2)[:, None]) & (slot[None, :] % 16 // 8 < counts[:, None])
    bias = jnp.where(jnp.repeat(live, BLK, axis=1), 0.0, NEG_FILL).astype(jnp.float32)

    query_rows = window_rows(queries[0], query_after)
    def column_halves(blocks):
        quarter = [pick(tensor_place ^ at, blocks) for at in range(4)]
        return [jnp.concatenate([quarter[k], quarter[2 + k]], axis=0) for k in range(2)]

    columns = column_halves(rounds)
    pair_columns = column_halves(pair_rounds)
    weight = out_weight.reshape(inner_dev, -1)
    grad_half = jnp.concatenate(columns, axis=1)
    partial_grad = lax.dot_general(
        grad_half, weight, (((1,), (1,)), ((), ())), preferred_element_type=jnp.float32
    ).reshape(2, rows, inner_dev)
    grad_own = jnp.where(dp_place == 0, partial_grad[0], partial_grad[1])
    grad_other = jnp.where(dp_place == 0, partial_grad[1], partial_grad[0]).astype(jnp.bfloat16)
    grad_context = (grad_own + flip_dp(grad_other).astype(jnp.float32)).astype(jnp.bfloat16)

    columns = [jnp.concatenate(both, axis=0) for both in zip(columns, pair_columns)]
    columns_own = jnp.where(core == 0, columns[0], columns[1])
    columns_other = flip_seq(jnp.where(core == 0, columns[1], columns[0]), 1)

    sent_back, context, grad_query = attend(bias, query_rows, grad_context, incoming)
    side = inner_dev // 2
    half_own = jnp.where(pair == 0, context[:, :side], context[:, side:])
    half_other = jnp.where(pair == 0, context[:, side:], context[:, :side])
    context_other = flip_dp(context)
    pair_own = flip_seq(half_other, 2)
    pair_other = moved(half_other, lambda s, t, d: (s ^ 2, t, 1 - d))
    sent_back, columns_own, columns_other = lax.optimization_barrier((sent_back, columns_own, columns_other))
    grad_blocks = lax.all_to_all(sent_back, SEQ, split_axis=0, concat_axis=0, tiled=True)

    def by_replica(own, other):
        return jnp.concatenate([jnp.where(dp_place == 0, own, other), jnp.where(dp_place == 0, other, own)], axis=0)

    context_both = by_replica(context, context_other)
    half_both = by_replica(half_own, jnp.where(pair == 0, context_other[:, :side], context_other[:, side:]))
    half_pair = jnp.concatenate([half_both, by_replica(pair_own, pair_other)], axis=0)
    context_group = jnp.concatenate([half_pair, flip_seq(half_pair, 1)], axis=0)
    grad_group = jnp.concatenate([columns_own, columns_other], axis=0)
    terms = lax.dot_general(context_group, grad_group, (((0,), (0,)), ((), ())), preferred_element_type=jnp.float32)
    terms, context_both = lax.optimization_barrier((terms.astype(jnp.bfloat16), context_both))
    terms = terms.reshape(side // HD, 8, HD // 8, -1)
    z = seq_place // 4
    parity = z % 2
    by_parity = terms.reshape(side // HD, 4, 2, HD // 8, -1)
    kept = jnp.where(parity == 0, by_parity[:, :, 0], by_parity[:, :, 1])
    given = jnp.where(parity == 0, by_parity[:, :, 1], by_parity[:, :, 0])
    middle = given.shape[-1] // 2
    came = jnp.concatenate(
        [
            moved(given[..., :middle], lambda s, t, d: (s + 4 if s // 4 % 2 == 0 else s - 4, t, d)),
            moved(given[..., middle:], lambda s, t, d: ((s - 4 if s // 4 % 2 == 0 else s + 4) % SHARDS, t, d)),
        ],
        axis=-1,
    )
    terms = (kept.astype(jnp.float32) + came.astype(jnp.float32)).astype(jnp.bfloat16)
    partial_out = jnp.dot(context_both, weight, preferred_element_type=jnp.float32).astype(jnp.bfloat16)
    width = partial_out.shape[1] // 2
    total = None
    for bits in range(4):
        piece = tensor_place ^ bits
        sent = lax.dynamic_slice(partial_out, (piece // 2 * rows, piece % 2 * width), (rows, width))
        came = (flip_tensor(sent, bits) if bits else sent).astype(jnp.float32)
        total = came if total is None else total + came
    total = total.astype(jnp.bfloat16)
    terms, grad_blocks, total = lax.optimization_barrier((terms, grad_blocks, total))
    out_own = moved(
        jnp.concatenate([total[:half], total[-BLK:]], axis=0), lambda s, t, d: (s, 2 * d + t % 2, t // 2)
    )
    out_before = moved(
        total[half:], lambda s, t, d: (s + 1, 2 * d + t % 2, t // 2) if s + 1 < SHARDS else None
    )
    summed = lax.dynamic_index_in_dim(terms, z // 2, axis=1, keepdims=False).astype(jnp.float32)
    for step in (2, 1, 3):
        sent = lax.dynamic_index_in_dim(terms, (z // 2 + step) % 4, axis=1, keepdims=False)
        came = moved(sent, lambda s, t, d, step=step: ((s + 8 * step) % SHARDS, t, d))
        summed = summed + came.astype(jnp.float32)
    grad_kv = unpack(block_target[0], grad_blocks)
    summed, grad_kv = lax.optimization_barrier((summed, grad_kv))
    summed, out_own, out_before = lax.optimization_barrier((summed, out_own, out_before))
    summed = summed.astype(jnp.bfloat16).reshape(side // HD, 4, HD // SHARDS, -1)
    place = 2 * pair + core
    quarters = [summed[:, at] for at in range(4)]
    received = [pick(place, quarters)] + [flip_seq(pick(place ^ bits, quarters), bits) for bits in (1, 2, 3)]
    by_pair = [jnp.concatenate([pick((2 * p + c) ^ place, received) for c in range(2)], axis=-1) for p in range(2)]
    weight_grad = jnp.concatenate(by_pair, axis=0).astype(jnp.float32)

    layer_out = token_rows(out_own, out_before)
    grad_queries = token_rows(grad_query, to_next(grad_query[half:]))

    return (layer_out[None], grad_queries[None], grad_kv[None], weight_grad)


def solution(mesh):
    fine = Mesh(mesh.devices.reshape(8, 2, 2, TENSOR, REPLICAS), AXES)
    in_specs = (
        P("dp", SEQ, "tensor"),
        P("dp", SEQ, None, "tensor"),
        P("dp", SEQ),
        P("dp", None),
        P("tensor", None, "dp"),
        P("dp", SEQ, "tensor"),
    )
    out_specs = (
        P("dp", SEQ, "tensor"),
        P("dp", SEQ, "tensor"),
        P("dp", SEQ, None, "tensor"),
        P("tensor", SEQ, "dp"),
    )
    return jax.shard_map(local, mesh=fine, in_specs=in_specs, out_specs=out_specs, check_vma=False)
```

```python
import jax
import jax.numpy as jnp
from jax import lax
from jax.experimental import pallas as pl
from jax.experimental.pallas import tpu as pltpu
from jax.sharding import Mesh, PartitionSpec as P

CLEN = 64
NLEN = 128
HD = 128
BLK = 16
SHARDS = 32
TENSOR = 4
REPLICAS = 2
NEG_FILL = -1e30
STEPS = 4
GROUP = 2
SEQ = ("z", "y", "core")
AXES = SEQ + ("tensor", "dp")
TAIL = 8


def moved(value, where):
    pairs = []
    for s in range(SHARDS):
        for t in range(TENSOR):
            for d in range(REPLICAS):
                to = where(s, t, d)
                if to is not None:
                    pairs.append(((s * TENSOR + t) * REPLICAS + d, (to[0] * TENSOR + to[1]) * REPLICAS + to[2]))
    return lax.ppermute(value, AXES, pairs)


def to_previous(value):
    return moved(value, lambda s, t, d: (s - 1, t, d) if s > 0 else None)


def to_next(value):
    return moved(value, lambda s, t, d: (s + 1, t, d) if s + 1 < SHARDS else None)


def flip_seq(value, bits):
    return moved(value, lambda s, t, d: (s ^ bits, t, d))


def flip_tensor(value, bits):
    return moved(value, lambda s, t, d: (s, t ^ bits, d))


def flip_dp(value):
    return moved(value, lambda s, t, d: (s, t, 1 - d))


def pick(index, options):
    chosen = options[-1]
    for at in range(len(options) - 2, -1, -1):
        chosen = jnp.where(index == at, options[at], chosen)
    return chosen


def window_rows(own, after):
    half = after.shape[0]
    last = lax.broadcasted_iota(jnp.int32, (half, 1), 0) == half - 1
    return jnp.concatenate([own[-half:], jnp.where(last, own[-half - 1 : -half], after)], axis=0)


def token_rows(own, before):
    half = before.shape[0]
    last = lax.broadcasted_iota(jnp.int32, (half, 1), 0) == half - 1
    return jnp.concatenate([jnp.where(last, own[-1:], before), own[:half]], axis=0)


def split_kernel(query_ref, grad_ref, query_first_ref, grad_first_ref, grad_last_ref):
    half = query_first_ref.shape[0]
    query_first_ref[...] = query_ref[:half, :]
    grad_first_ref[...] = grad_ref[:half, :]
    grad_last_ref[...] = grad_ref[half - BLK :, :]


def split(query, grad):
    rows, width = query.shape
    vmem = pl.BlockSpec(memory_space=pltpu.VMEM)
    return pl.pallas_call(
        split_kernel,
        in_specs=[vmem] * 2,
        out_specs=[vmem] * 3,
        out_shape=[
            jax.ShapeDtypeStruct((size, width), jnp.bfloat16) for size in (rows // 2, rows // 2, rows // 2 + BLK)
        ],
        compiler_params=pltpu.CompilerParams(vmem_limit_bytes=56 * 1024 * 1024),
        cost_estimate=pl.CostEstimate(flops=0, bytes_accessed=16 * rows * width, transcendentals=0),
    )(query, grad)


def pack_kernel(target_ref, rows_ref, out_ref):
    step = pl.program_id(0)
    heads = rows_ref.shape[2] // HD
    blocks = rows_ref.shape[0] // BLK
    for at in range(blocks):
        target = target_ref[step * blocks + at]
        place = target // SHARDS
        for head in range(heads):
            pair = jnp.transpose(rows_ref[at * BLK : (at + 1) * BLK, :, head * HD : (head + 1) * HD], (1, 0, 2))
            row = 2 * BLK * head
            out_ref[place, row : row + BLK, :] = pair[0]
            out_ref[place, row + BLK : row + 2 * BLK, :] = pair[1]
        slot = jnp.full((TAIL, HD), target % SHARDS, jnp.int32)
        out_ref[place, 2 * BLK * heads :, :] = slot.astype(jnp.float32).astype(jnp.bfloat16)


def pack(target, rows):
    total, _, width = rows.shape
    out_rows = 2 * BLK * (width // HD) + TAIL
    return pl.pallas_call(
        pack_kernel,
        grid=(STEPS,),
        in_specs=[
            pl.BlockSpec(memory_space=pltpu.SMEM),
            pl.BlockSpec((total // STEPS, 2, width), lambda step: (step, 0, 0)),
        ],
        out_specs=pl.BlockSpec((SHARDS, out_rows, HD), lambda step: (0, 0, 0)),
        out_shape=jax.ShapeDtypeStruct((SHARDS, out_rows, HD), jnp.bfloat16),
        compiler_params=pltpu.CompilerParams(vmem_limit_bytes=56 * 1024 * 1024),
        cost_estimate=pl.CostEstimate(flops=0, bytes_accessed=16 * rows.size, transcendentals=0),
    )(target, rows)


def unpack_kernel(target_ref, part_ref, out_ref):
    step = pl.program_id(0)
    heads = out_ref.shape[2] // HD
    blocks = out_ref.shape[0] // BLK
    for at in range(blocks):
        source = target_ref[step * blocks + at] // SHARDS
        for head in range(heads):
            row = 2 * BLK * head
            both = part_ref[source, row : row + 2 * BLK, :].reshape(2, BLK, HD)
            out_ref[at * BLK : (at + 1) * BLK, :, head * HD : (head + 1) * HD] = jnp.transpose(both, (1, 0, 2))


def unpack(target, part):
    total, width = SHARDS * BLK, part.shape[1] // (2 * BLK) * HD
    return pl.pallas_call(
        unpack_kernel,
        grid=(STEPS,),
        in_specs=[
            pl.BlockSpec(memory_space=pltpu.SMEM),
            pl.BlockSpec(part.shape, lambda step: (0, 0, 0)),
        ],
        out_specs=pl.BlockSpec((total // STEPS, 2, width), lambda step: (step, 0, 0)),
        out_shape=jax.ShapeDtypeStruct((total, 2, width), jnp.bfloat16),
        compiler_params=pltpu.CompilerParams(vmem_limit_bytes=32 * 1024 * 1024),
        cost_estimate=pl.CostEstimate(flops=0, bytes_accessed=16 * total * width, transcendentals=0),
    )(target, part)


def attend_kernel(count_ref, slot_ref, query_ref, grad_ref, kv_ref, grad_kv_ref, context_ref, grad_query_ref):
    rows = query_ref.shape[0]
    heads = query_ref.shape[1] // HD
    blocks = kv_ref.shape[0]
    keys = blocks * BLK
    scale = HD ** (-0.5)
    row = lax.broadcasted_iota(jnp.int32, (rows, 1), 0)
    second = (row >= CLEN - 1) & (row < rows - 1)
    block = lax.broadcasted_iota(jnp.int32, (blocks, keys), 0)
    own = (lax.broadcasted_iota(jnp.int32, (blocks, keys), 1) >> 4) == block
    spread = jnp.where(own, 1.0, 0.0).astype(jnp.bfloat16)
    slot = lax.dot_general(slot_ref[...], spread, (((0,), (0,)), ((), ())), preferred_element_type=jnp.float32)
    low_slot = jnp.where(second, 16, 0)
    high_slot = low_slot + 8 * jnp.where(second, count_ref[1], count_ref[0])
    live = (slot >= low_slot.astype(jnp.float32)) & (slot < high_slot.astype(jnp.float32))
    bias = jnp.where(live, 0.0, NEG_FILL)
    nt = (((1,), (1,)), ((), ()))
    tn = (((0,), (0,)), ((), ()))
    for head in range(heads):
        lanes = slice(head * HD, (head + 1) * HD)
        first, middle, last = 2 * BLK * head, 2 * BLK * head + BLK, 2 * BLK * (head + 1)
        query = query_ref[:, lanes]
        grad = grad_ref[:, lanes]
        key = kv_ref[:, first:middle, :].reshape(keys, HD)
        value = kv_ref[:, middle:last, :].reshape(keys, HD)
        scores = lax.dot_general(query, key, nt, preferred_element_type=jnp.float32) * scale + bias
        raw = jnp.exp(scores - jnp.max(scores, axis=-1, keepdims=True))
        soft = raw * (1.0 / jnp.sum(raw, axis=-1, keepdims=True))
        low = soft.astype(jnp.bfloat16)
        context = jnp.dot(low, value, preferred_element_type=jnp.float32).astype(jnp.bfloat16)
        context_ref[:, lanes] = context
        grad_weights = lax.dot_general(grad, value, nt, preferred_element_type=jnp.float32)
        delta = jnp.sum(grad.astype(jnp.float32) * context.astype(jnp.float32), axis=-1, keepdims=True)
        grad_scores = (soft * (grad_weights - delta) * scale).astype(jnp.bfloat16)
        grad_query = jnp.dot(grad_scores, key, preferred_element_type=jnp.float32)
        grad_query_ref[:, lanes] = grad_query.astype(jnp.bfloat16)
        grad_key = lax.dot_general(grad_scores, query, tn, preferred_element_type=jnp.float32)
        grad_value = lax.dot_general(low, grad, tn, preferred_element_type=jnp.float32)
        grad_kv_ref[:, first:middle, :] = grad_key.astype(jnp.bfloat16).reshape(blocks, BLK, HD)
        grad_kv_ref[:, middle:last, :] = grad_value.astype(jnp.bfloat16).reshape(blocks, BLK, HD)


def attend(counts, slots, query, grad, kv):
    rows, width = query.shape
    blocks = kv.shape[0]
    keys = blocks * BLK
    heads = width // HD
    per_head = pl.BlockSpec((rows, GROUP * HD), lambda h: (0, h))
    block_spec = pl.BlockSpec((blocks, GROUP * 2 * BLK, HD), lambda h: (0, h, 0))
    return pl.pallas_call(
        attend_kernel,
        grid=(heads // GROUP,),
        in_specs=[
            pl.BlockSpec(memory_space=pltpu.SMEM),
            pl.BlockSpec(slots.shape, lambda h: (0, 0)),
            per_head,
            per_head,
            block_spec,
        ],
        out_specs=[block_spec, per_head, per_head],
        out_shape=[
            jax.ShapeDtypeStruct((blocks, 2 * BLK * heads, HD), jnp.bfloat16),
            jax.ShapeDtypeStruct((rows, width), jnp.bfloat16),
            jax.ShapeDtypeStruct((rows, width), jnp.bfloat16),
        ],
        compiler_params=pltpu.CompilerParams(vmem_limit_bytes=56 * 1024 * 1024),
        cost_estimate=pl.CostEstimate(
            flops=heads * 12 * rows * keys * HD,
            bytes_accessed=4 * kv.size + 8 * rows * width,
            transcendentals=heads * rows * keys,
        ),
    )(counts, slots, query, grad, kv)


def local(queries, neighbour_kv, block_target, neighbour_count, out_weight, grad_mixed):
    seq_place = lax.axis_index(SEQ)
    tensor_place = lax.axis_index("tensor")
    dp_place = lax.axis_index("dp")
    core = seq_place % 2
    pair = (seq_place // 2) % 2
    rows, inner_dev = queries.shape[1:]
    heads_dev = inner_dev // HD

    half = rows // 2
    query_first, grad_first, grad_last = split(queries[0], grad_mixed[0])
    query_after = to_previous(query_first)
    grad_own = moved(grad_last, lambda s, t, d: (s, 2 * d + t % 2, t // 2))
    grad_after = moved(
        grad_first, lambda s, t, d: (s - 1, 2 * d + t % 2, t // 2) if s > 0 else None
    )
    packed = pack(block_target[0], neighbour_kv[0])
    packed, grad_own, grad_after, query_after = lax.optimization_barrier((packed, grad_own, grad_after, query_after))
    incoming = lax.all_to_all(packed, SEQ, split_axis=0, concat_axis=0, tiled=True)
    grad_rows = window_rows(grad_own, grad_after)
    rounds = [grad_rows] + [flip_tensor(grad_rows, bits) for bits in (1, 2, 3)]
    pair_rows = flip_seq(grad_rows, 2)
    pair_rows, rounds = lax.optimization_barrier((pair_rows, rounds))
    pair_rounds = [pair_rows] + [flip_tensor(pair_rows, bits) for bits in (1, 2, 3)]
    slots = incoming[:, -TAIL, :]
    counts = lax.dynamic_slice(neighbour_count[0], (2 * seq_place,), (2,))

    query_rows = window_rows(queries[0], query_after)
    def column_halves(blocks):
        quarter = [pick(tensor_place ^ at, blocks) for at in range(4)]
        return [jnp.concatenate([quarter[k], quarter[2 + k]], axis=0) for k in range(2)]

    columns = column_halves(rounds)
    pair_columns = column_halves(pair_rounds)
    weight = out_weight.reshape(inner_dev, -1)
    grad_half = jnp.concatenate(columns, axis=1)
    partial_grad = lax.dot_general(
        grad_half, weight, (((1,), (1,)), ((), ())), preferred_element_type=jnp.float32
    ).reshape(2, rows, inner_dev)
    grad_own = jnp.where(dp_place == 0, partial_grad[0], partial_grad[1])
    grad_other = jnp.where(dp_place == 0, partial_grad[1], partial_grad[0]).astype(jnp.bfloat16)
    grad_context = (grad_own + flip_dp(grad_other).astype(jnp.float32)).astype(jnp.bfloat16)

    columns = [jnp.concatenate(both, axis=0) for both in zip(columns, pair_columns)]
    columns_own = jnp.where(core == 0, columns[0], columns[1])
    columns_other = flip_seq(jnp.where(core == 0, columns[1], columns[0]), 1)

    sent_back, context, grad_query = attend(counts, slots, query_rows, grad_context, incoming)
    side = inner_dev // 2
    half_own = jnp.where(pair == 0, context[:, :side], context[:, side:])
    half_other = jnp.where(pair == 0, context[:, side:], context[:, :side])
    context_other = flip_dp(context)
    pair_own = flip_seq(half_other, 2)
    pair_other = moved(half_other, lambda s, t, d: (s ^ 2, t, 1 - d))
    sent_back, columns_own, columns_other = lax.optimization_barrier((sent_back, columns_own, columns_other))
    grad_blocks = lax.all_to_all(sent_back, SEQ, split_axis=0, concat_axis=0, tiled=True)

    def by_replica(own, other):
        return jnp.concatenate([jnp.where(dp_place == 0, own, other), jnp.where(dp_place == 0, other, own)], axis=0)

    context_both = by_replica(context, context_other)
    half_both = by_replica(half_own, jnp.where(pair == 0, context_other[:, :side], context_other[:, side:]))
    half_pair = jnp.concatenate([half_both, by_replica(pair_own, pair_other)], axis=0)
    context_group = jnp.concatenate([half_pair, flip_seq(half_pair, 1)], axis=0)
    grad_group = jnp.concatenate([columns_own, columns_other], axis=0)
    terms = lax.dot_general(context_group, grad_group, (((0,), (0,)), ((), ())), preferred_element_type=jnp.float32)
    terms, context_both = lax.optimization_barrier((terms.astype(jnp.bfloat16), context_both))
    terms = terms.reshape(side // HD, 8, HD // 8, -1)
    z = seq_place // 4
    parity = z % 2
    by_parity = terms.reshape(side // HD, 4, 2, HD // 8, -1)
    kept = jnp.where(parity == 0, by_parity[:, :, 0], by_parity[:, :, 1])
    given = jnp.where(parity == 0, by_parity[:, :, 1], by_parity[:, :, 0])
    middle = given.shape[-1] // 2
    came = jnp.concatenate(
        [
            moved(given[..., :middle], lambda s, t, d: (s + 4 if s // 4 % 2 == 0 else s - 4, t, d)),
            moved(given[..., middle:], lambda s, t, d: ((s - 4 if s // 4 % 2 == 0 else s + 4) % SHARDS, t, d)),
        ],
        axis=-1,
    )
    terms = (kept.astype(jnp.float32) + came.astype(jnp.float32)).astype(jnp.bfloat16)
    partial_out = jnp.dot(context_both, weight, preferred_element_type=jnp.float32).astype(jnp.bfloat16)
    width = partial_out.shape[1] // 2
    total = None
    for bits in range(4):
        piece = tensor_place ^ bits
        sent = lax.dynamic_slice(partial_out, (piece // 2 * rows, piece % 2 * width), (rows, width))
        came = (flip_tensor(sent, bits) if bits else sent).astype(jnp.float32)
        total = came if total is None else total + came
    total = total.astype(jnp.bfloat16)
    terms, grad_blocks, total = lax.optimization_barrier((terms, grad_blocks, total))
    out_own = moved(
        jnp.concatenate([total[:half], total[-BLK:]], axis=0), lambda s, t, d: (s, 2 * d + t % 2, t // 2)
    )
    out_before = moved(
        total[half:], lambda s, t, d: (s + 1, 2 * d + t % 2, t // 2) if s + 1 < SHARDS else None
    )
    summed = lax.dynamic_index_in_dim(terms, z // 2, axis=1, keepdims=False).astype(jnp.float32)
    for step in (2, 1, 3):
        sent = lax.dynamic_index_in_dim(terms, (z // 2 + step) % 4, axis=1, keepdims=False)
        came = moved(sent, lambda s, t, d, step=step: ((s + 8 * step) % SHARDS, t, d))
        summed = summed + came.astype(jnp.float32)
    grad_kv = unpack(block_target[0], grad_blocks)
    summed, grad_kv = lax.optimization_barrier((summed, grad_kv))
    summed, out_own, out_before = lax.optimization_barrier((summed, out_own, out_before))
    summed = summed.astype(jnp.bfloat16).reshape(side // HD, 4, HD // SHARDS, -1)
    place = 2 * pair + core
    quarters = [summed[:, at] for at in range(4)]
    received = [pick(place, quarters)] + [flip_seq(pick(place ^ bits, quarters), bits) for bits in (1, 2, 3)]
    by_pair = [jnp.concatenate([pick((2 * p + c) ^ place, received) for c in range(2)], axis=-1) for p in range(2)]
    weight_grad = jnp.concatenate(by_pair, axis=0).astype(jnp.float32)

    layer_out = token_rows(out_own, out_before)
    grad_queries = token_rows(grad_query, to_next(grad_query[half:]))

    return (layer_out[None], grad_queries[None], grad_kv[None], weight_grad)


def solution(mesh):
    fine = Mesh(mesh.devices.reshape(8, 2, 2, TENSOR, REPLICAS), AXES)
    in_specs = (
        P("dp", SEQ, "tensor"),
        P("dp", SEQ, None, "tensor"),
        P("dp", SEQ),
        P("dp", None),
        P("tensor", None, "dp"),
        P("dp", SEQ, "tensor"),
    )
    out_specs = (
        P("dp", SEQ, "tensor"),
        P("dp", SEQ, "tensor"),
        P("dp", SEQ, None, "tensor"),
        P("tensor", SEQ, "dp"),
    )
    return jax.shard_map(local, mesh=fine, in_specs=in_specs, out_specs=out_specs, check_vma=False)
```
